256 devices in a mesh: prow: 16 (over z_lo, x), pcol: 16 (over z_hi, y, core).
Axes of the slice: x: 4, y: 4, z: 8 (z_hi: 2, z_lo: 4; z = z_hi * 4 + z_lo), core: 2. Of those that a mesh axis runs over, the one named last changes fastest.
Arguments:
- features: bfloat16 [65536, 1024], P('prow', 'pcol'), may hold values from -6 to 6
- panel_offsets: int32 [2], replicated, may hold values from 0 to 480, as said below
- length_scale: float32 [1], replicated, may hold values from 30 to 60
- variance: float32 [1], replicated, may hold values from 0.5 to 2
Outputs:
- panels: float32 [2, 65536, 4096], P(None, 'prow', 'pcol')
The draws below stay inside these ranges and needn't reach their ends.
Inputs may be any that keep to these rules, and one draw needn't show every extreme that they name: panel_offsets[1] is 480 and panel_offsets[0] is smaller; a panel stays inside the matrix.
All inputs are finite; a program needn't handle non-finite values.
Results may differ from the reference program's by a relative error of at most 0.0003.
Values may be sent and summed in bfloat16 or wider, within the bound.
A program may use at most 128 MiB of HBM per device.

```python
import jax
import jax.numpy as jnp
from jax import lax

F = 1024
TB = 128
PT = 32
ROWS_DEV = 4096
NPTS = 65536
NTILES = 512
N_PROW = 16
N_PCOL = 16


def draw_panel_offsets(key, part):
    key = jax.random.fold_in(key, 7)
    first = jax.random.randint(key, (1,), 0, NTILES - PT)
    last = jnp.full((1,), NTILES - PT, jnp.int32)
    return jnp.concatenate([first.astype(jnp.int32), last])


def block_levels(rng, shape, split, smallest, high):
    factor_of, own = 1.0, jax.random.fold_in(rng, 6)
    for axis_at, shards_of in split:
        steps = jnp.exp(jax.random.uniform(jax.random.fold_in(own, axis_at), (shards_of,), jnp.float32, smallest / len(split), high / len(split)))
        factor_of = factor_of * jnp.repeat(steps, shape[axis_at] // shards_of).reshape([-1 if axis == axis_at else 1 for axis in range(len(shape))])
    return factor_of


def centred(rng, shape, scale, reach, cuts=(), held_as=jnp.bfloat16):
    entries = scale * jax.random.normal(rng, shape, jnp.float32)
    if cuts:
        entries = entries * block_levels(rng, shape, cuts, -0.22, 0.18)
    return jnp.clip(entries, -reach, reach).astype(held_as)


def setup_inputs(seed: int = 0) -> dict:
    arg_keys = jax.random.split(jax.random.key(seed), 5)
    features = centred(arg_keys[0], (NPTS, F), 1.0, 6.0, ((0, 16), (1, 16)))
    panel_offsets = draw_panel_offsets(jax.random.fold_in(arg_keys[4], 71), 0)
    length_scale = jnp.clip(jax.random.uniform(arg_keys[2], (1,), jnp.float32, 30.0, 60.0), 30.0, 60.0)
    variance = jnp.clip(jax.random.uniform(arg_keys[3], (1,), jnp.float32, 0.5, 2.0), 0.5, 2.0)
    return {"features": features, "panel_offsets": panel_offsets, "length_scale": length_scale, "variance": variance}


def matern(sq_dist, length_scale, variance):
    scaled = 5.0 * sq_dist / (length_scale[0] * length_scale[0])
    dist_a = jnp.sqrt(scaled)
    return variance[0] * (1.0 + dist_a + scaled / 3.0) * jnp.exp(-dist_a)

def reference(features, panel_offsets, length_scale, variance):
    total = features.shape[0]
    steps = ROWS_DEV // TB
    points = features.reshape(N_PROW, steps, TB, F).transpose(1, 0, 2, 3).reshape(total, F)

    def panel_cols(offset):
        picked = lax.dynamic_slice_in_dim(points, (offset * TB).astype(jnp.int32), PT * TB, 0)
        return picked.reshape(PT // N_PCOL, N_PCOL, TB, F).transpose(1, 0, 2, 3).reshape(PT * TB, F)
    columns = jnp.concatenate([panel_cols(panel_offsets[0]), panel_cols(panel_offsets[1])], 0)
    col_norm = lax.optimization_barrier(jnp.sum(jnp.square(columns.astype(jnp.float32)), axis=1))
    blocks = features.reshape(N_PROW, ROWS_DEV, F)

    def one_block(rows_block):
        gram = jnp.dot(rows_block, columns.T, preferred_element_type=jnp.float32)
        row_norm = lax.optimization_barrier(jnp.sum(jnp.square(rows_block.astype(jnp.float32)), axis=1))
        sq_dist = jnp.maximum(row_norm[:, None] + col_norm[None, :] - 2.0 * gram, 0.0)
        return matern(sq_dist, length_scale, variance)
    kernel = lax.map(one_block, blocks).reshape(total, 2, PT * TB)
    return kernel.transpose(1, 0, 2)
```

```python
import functools

import jax
import jax.numpy as jnp
from jax import lax
from jax.experimental import pallas as pl
from jax.experimental.pallas import tpu as pltpu
from jax.sharding import PartitionSpec as P

TB = 128
NC = 8
LOG2E = 1.4426950408889634
MESH = pl.DeviceIdType.MESH
BF16 = jnp.bfloat16
F32 = jnp.float32


def pick(options, which):
    which = jnp.full(options[0].shape, which, jnp.int32)
    out = options[0].astype(F32)
    for n, option in enumerate(options[1:], 1):
        out = jnp.where(which == n, option.astype(F32), out)
    return out.astype(BF16)


def kernel(off_ref, ls_ref, var_ref, x_hbm, o_ref, xv, tr, rows, cols, rot1, rot2, mine, cnorm,
           in_sem, s_sw, r_sw, s_row, r_row, s_sib, r_sib, s_rot, r_rot, s_tp, r_tp, s_cz, r_cz, s_cx, r_cx):
    r = lax.axis_index("prow")
    q = lax.axis_index("pcol")
    x = r % 4
    zl = r // 4
    c = q % 2
    oc = 1 - c
    y = (q // 2) % 4
    zh = q // 8
    rc = rows.shape[3]
    hc = rc // 2
    half = NC * rc

    def at_q(zhi, yy, cc):
        return {"prow": r, "pcol": zhi * 8 + yy * 2 + cc}

    def at_r(rr):
        return {"prow": rr, "pcol": q}

    sib = at_q(zh, y, oc)
    up = at_q(zh, (y + 1) % 4, c)
    down = at_q(zh, (y + 3) % 4, c)
    across = at_q(1 - zh, y, c)
    flip = {"prow": q, "pcol": r}

    load = pltpu.make_async_copy(x_hbm, xv, in_sem)
    load.start()
    bar = pltpu.get_barrier_semaphore()
    for d in (sib, up, down, across):
        pl.semaphore_signal(bar, inc=1, device_id=d, device_id_type=MESH)
    for d in range(1, 16):
        pl.semaphore_signal(bar, inc=1, device_id=at_r((r + d) % 16), device_id_type=MESH)

    @pl.when(q != r)
    def _():
        pl.semaphore_signal(bar, inc=1, device_id=flip, device_id_type=MESH)

    load.wait()
    off0 = off_ref[0]
    slot = lax.shift_right_logical(off0 - r + 15, 4)
    rot1[0] = pick([xv[:, s * TB:(s + 2) * TB] for s in range(xv.shape[1] // TB - 1)], slot)
    mine[1] = xv[:, xv.shape[1] - 2 * TB:]
    pl.semaphore_wait(bar, 19 + (q != r).astype(jnp.int32))

    def swap(i):
        return pltpu.make_async_remote_copy(
            xv.at[:, pl.ds(pl.multiple_of(oc * half + i * rc, rc), rc)], tr.at[i, c],
            s_sw.at[i], r_sw.at[i], device_id=sib, device_id_type=MESH)

    @pl.loop(0, NC)
    def _(i):
        swap(i).start()

    def turn(stage, d):
        buf = rot1 if stage == 0 else rot2
        step = 1 if stage == 0 else 4
        return pltpu.make_async_remote_copy(
            buf.at[0], buf.at[d], s_rot.at[stage, d - 1], r_rot.at[stage, d - 1],
            device_id=at_r((r + 16 - step * d) % 16), device_id_type=MESH)

    def flipped(p):
        return pltpu.make_async_remote_copy(
            mine.at[p], cols.at[p, zh * 2 + y // 2, (y % 2) * 2 + c], s_tp.at[p], r_tp.at[p],
            device_id=flip, device_id_type=MESH)

    def flip_start(p):
        @pl.when(q != r)
        def _():
            flipped(p).start()

        @pl.when(q == r)
        def _():
            cols[p, zl, x] = mine[p]

    def flip_wait(p):
        @pl.when(q != r)
        def _():
            flipped(p).wait_recv()

    def col_z(p, d):
        return pltpu.make_async_remote_copy(
            cols.at[p, zl, x], cols.at[p, zl, x], s_cz.at[p, d - 1], r_cz.at[p, d - 1],
            device_id=at_r((r + 4 * d) % 16), device_id_type=MESH)

    def col_z_wait(p, d):
        src = cols.at[p, (zl + 4 - d) % 4, x]
        return pltpu.make_async_remote_copy(
            src, src, s_cz.at[p, d - 1], r_cz.at[p, d - 1],
            device_id=at_r((r + 4 * d) % 16), device_id_type=MESH)

    def col_x(p, d):
        return pltpu.make_async_remote_copy(
            cols.at[p, :, x], cols.at[p, :, x], s_cx.at[p, d - 1], r_cx.at[p, d - 1],
            device_id=at_r(zl * 4 + (x + d) % 4), device_id_type=MESH)

    def col_x_wait(p, d):
        src = cols.at[p, :, (x + 4 - d) % 4]
        return pltpu.make_async_remote_copy(
            src, src, s_cx.at[p, d - 1], r_cx.at[p, d - 1],
            device_id=at_r(zl * 4 + (x + d) % 4), device_id_type=MESH)

    for d in (1, 2, 3):
        turn(0, d).start()
    flip_start(1)

    UP, DOWN, FUP, FDOWN, ACROSS = 0, 1, 2, 3, 8

    def base(g):
        return (zh if g == 0 else 1 - zh) * 4

    def row_copy(kind, i, block, lo, n, to):
        ref = rows.at[c, i, block, pl.ds(lo, n)]
        return pltpu.make_async_remote_copy(ref, ref, s_row.at[kind, i], r_row.at[kind, i],
                                            device_id=to, device_id_type=MESH)

    def send_up(g, i):
        return row_copy(4 * g + UP, i, base(g) + y, 0, rc, up)

    def send_down(g, i):
        return row_copy(4 * g + DOWN, i, base(g) + y, 0, rc, down)

    def send_across(i):
        return row_copy(ACROSS, i, base(0) + y, 0, rc, across)

    def pass_up(g, i):
        return row_copy(4 * g + FUP, i, base(g) + (y + 3) % 4, 0, hc, up)

    def pass_down(g, i):
        return row_copy(4 * g + FDOWN, i, base(g) + (y + 1) % 4, hc, hc, down)

    def got_up(g, i):
        return row_copy(4 * g + UP, i, base(g) + (y + 3) % 4, 0, rc, up)

    def got_down(g, i):
        return row_copy(4 * g + DOWN, i, base(g) + (y + 1) % 4, 0, rc, down)

    def got_across(i):
        return row_copy(ACROSS, i, base(1) + y, 0, rc, across)

    def got_pass_up(g, i):
        return row_copy(4 * g + FUP, i, base(g) + (y + 2) % 4, 0, hc, up)

    def got_pass_down(g, i):
        return row_copy(4 * g + FDOWN, i, base(g) + (y + 2) % 4, hc, hc, down)

    def share(g, i, h):
        ref = rows.at[h, i, pl.ds(base(g), 4)]
        return pltpu.make_async_remote_copy(ref, ref, s_sib.at[g, i], r_sib.at[g, i],
                                            device_id=sib, device_id_type=MESH)

    own = zh * 4 + y

    @pl.loop(0, NC)
    def _(i):
        tr[i, c] = xv[:, pl.ds(pl.multiple_of(c * half + i * rc, rc), rc)]
        pltpu.make_async_remote_copy(tr.at[i, oc], tr.at[i, oc], s_sw.at[i], r_sw.at[i],
                                     device_id=sib, device_id_type=MESH).wait_recv()
        rows[c, i, own] = tr[i].reshape(2 * tr.shape[2], rc).T
        send_across(i).start()
        send_up(0, i).start()
        send_down(0, i).start()

    for d in (1, 2, 3):
        turn(0, d).wait_recv()
    rot2[0] = pick([rot1[d] for d in range(4)], lax.bitwise_and(off0, 3))
    for d in (1, 2, 3):
        turn(1, d).start()

    def columns(step):
        if step == 0:
            flip_wait(1)
            for d in (1, 2, 3):
                col_z(1, d).start()
            for d in (1, 2, 3):
                turn(1, d).wait_recv()
            mine[0] = pick([rot2[d] for d in range(4)], lax.bitwise_and(lax.shift_right_logical(off0, 2), 3))
            flip_start(0)
        if step == 1:
            for d in (1, 2, 3):
                col_z_wait(1, d).wait_recv()
            for d in (1, 2, 3):
                col_x(1, d).start()
        if step == 2:
            flip_wait(0)
            for d in (1, 2, 3):
                col_z(0, d).start()
        if step == 3:
            for d in (1, 2, 3):
                col_z_wait(0, d).wait_recv()
            for d in (1, 2, 3):
                col_x(0, d).start()

    def stage_a(i):
        got_across(i).wait_recv()
        send_up(1, i).start()
        send_down(1, i).start()
        got_up(0, i).wait_recv()
        pass_up(0, i).start()
        got_down(0, i).wait_recv()
        pass_down(0, i).start()

    def stage_b(i):
        got_up(1, i).wait_recv()
        pass_up(1, i).start()
        got_down(1, i).wait_recv()
        pass_down(1, i).start()
        got_pass_up(0, i).wait_recv()
        got_pass_down(0, i).wait_recv()
        share(0, i, c).start()

    def stage_c(i):
        got_pass_up(1, i).wait_recv()
        got_pass_down(1, i).wait_recv()
        share(1, i, c).start()

    ls = ls_ref[0]
    var = var_ref[0]
    scale = 5.0 / (ls * ls)

    def norms():
        for p in (0, 1):
            for d in (1, 2, 3):
                col_x_wait(p, d).wait_recv()
            total = jnp.zeros((1, 2 * TB), F32)
            for a in range(4):
                for b in range(4):
                    total += jnp.sum(jnp.square(cols[p, a, b].astype(F32)), axis=0, keepdims=True)
            cnorm[p] = total

    def compute(h, i):
        lhs = jnp.concatenate([rows[h, i, k] for k in range(8)], axis=1)
        rn = jnp.sum(jnp.square(lhs.astype(F32)), axis=1, keepdims=True)
        for p in (0, 1):
            rhs = cols[p].reshape(lhs.shape[1], 2 * TB)
            gram = jnp.dot(lhs, rhs, preferred_element_type=F32)
            sq = jnp.maximum((rn + cnorm[p] - 2.0 * gram) * scale, 1e-30)
            dist = sq * lax.rsqrt(sq)
            out = (var * (1.0 + dist + sq * (1.0 / 3.0))) * jnp.exp2(dist * (-LOG2E))
            o_ref[p, pl.ds(pl.multiple_of(h * half + i * rc, rc), rc), :] = out

    def stage_d(i):
        share(0, i, oc).wait_recv()
        share(1, i, oc).wait_recv()

        @pl.loop(0, 2)
        def _(h):
            compute(h, i)

    LB, LC, LD = 4, 5, 6
    for i in range(4):
        columns(i)
        stage_a(i)

    @pl.loop(4, 5)
    def _(i):
        stage_a(i)
        stage_b(i - LB)

    @pl.loop(5, 6)
    def _(i):
        stage_a(i)
        stage_b(i - LB)
        stage_c(i - LC)

    norms()

    @pl.loop(6, NC)
    def _(i):
        stage_a(i)
        stage_b(i - LB)
        stage_c(i - LC)
        stage_d(i - LD)

    @pl.loop(NC, NC + 4)
    def _(i):
        stage_b(i - LB)
        stage_c(i - LC)
        stage_d(i - LD)

    @pl.loop(NC + 4, NC + 5)
    def _(i):
        stage_c(i - LC)
        stage_d(i - LD)

    @pl.loop(NC + 5, NC + 6)
    def _(i):
        stage_d(i - LD)

    for stage in (0, 1):
        for d in (1, 2, 3):
            turn(stage, d).wait_send()
    for p in (0, 1):
        @pl.when(q != r)
        def _():
            flipped(p).wait_send()

        for d in (1, 2, 3):
            col_z(p, d).wait_send()
            col_x(p, d).wait_send()

    @pl.loop(0, NC)
    def _(i):
        swap(i).wait_send()
        send_across(i).wait_send()
        for g in (0, 1):
            send_up(g, i).wait_send()
            send_down(g, i).wait_send()
            pass_up(g, i).wait_send()
            pass_down(g, i).wait_send()
            share(g, i, c).wait_send()


def on_device(features, panel_offsets, length_scale, variance):
    pts, width = features.shape
    rc = pts // (2 * NC)
    smem = pl.BlockSpec(memory_space=pltpu.SMEM)
    dma = pltpu.SemaphoreType.DMA
    return pl.pallas_call(
        kernel,
        out_shape=pltpu.VMEM((2, pts, 2 * TB), F32),
        in_specs=[smem, smem, smem, pl.BlockSpec(memory_space=pl.ANY)],
        out_specs=pl.BlockSpec(memory_space=pltpu.VMEM),
        scratch_shapes=[
            pltpu.VMEM((width, pts), BF16),
            pltpu.VMEM((NC, 2, width, rc), BF16),
            pltpu.VMEM((2, NC, 8, rc, 2 * width), BF16),
            pltpu.VMEM((2, 4, 4, width, 2 * TB), BF16),
            pltpu.VMEM((4, width, 2 * TB), BF16),
            pltpu.VMEM((4, width, 2 * TB), BF16),
            pltpu.VMEM((2, width, 2 * TB), BF16),
            pltpu.VMEM((2, 1, 2 * TB), F32),
            dma, dma((NC,)), dma((NC,)), dma((9, NC)), dma((9, NC)), dma((2, NC)), dma((2, NC)),
            dma((2, 3)), dma((2, 3)), dma((2,)), dma((2,)), dma((2, 3)), dma((2, 3)), dma((2, 3)), dma((2, 3)),
        ],
        compiler_params=pltpu.CompilerParams(
            collective_id=0, has_side_effects=True, vmem_limit_bytes=48 * 2**20),
        cost_estimate=pl.CostEstimate(flops=2 * pts * 1024 * 512, bytes_accessed=9 * 2**20, transcendentals=0),
        name="panels",
    )(panel_offsets, length_scale, variance, features.T)


def solution(mesh):
    return jax.shard_map(
        on_device,
        mesh=mesh,
        in_specs=(P("prow", "pcol"), P(), P(), P()),
        out_specs=P(None, "prow", "pcol"),
        check_vma=False,
    )
```

```python
import functools

import jax
import jax.numpy as jnp
from jax import lax
from jax.experimental import pallas as pl
from jax.experimental.pallas import tpu as pltpu
from jax.sharding import PartitionSpec as P

TB = 128
NC = 8
AHEAD = 8
LAG = (2, 3, 4, 5)
ZWIN = 3
EARLY = (-1, 0)
OWN = (3, 3, 6, 8)
STEPS = (2, 4, 7)
CS1 = 7
LOG2E = 1.4426950408889634
MESH = pl.DeviceIdType.MESH
BF16 = jnp.bfloat16
F32 = jnp.float32


def pick(options, which):
    which = jnp.full(options[0].shape, which, jnp.int32)
    out = options[0].astype(F32)
    for n, option in enumerate(options[1:], 1):
        out = jnp.where(which == n, option.astype(F32), out)
    return out.astype(BF16)


def gathered(rows, i):
    return jnp.concatenate([
        jnp.concatenate([rows[h, i, k] for k in range(8)], axis=1) for h in (0, 1)], axis=0)


def col_norm(cols, p):
    total = jnp.zeros((1, 2 * TB), F32)
    for a in range(4):
        for b in range(4):
            total += jnp.sum(jnp.square(cols[p, a, b].astype(F32)), axis=0, keepdims=True)
    return total


def values(lhs, rn, columns, cn, scale, var):
    gram = jnp.dot(lhs, columns.reshape(lhs.shape[1], 2 * TB), preferred_element_type=F32)
    sq = jnp.maximum((rn + cn - 2.0 * gram) * scale, 1e-30)
    dist = sq * lax.rsqrt(sq)
    return (var * (1.0 + dist + sq * (1.0 / 3.0))) * jnp.exp2(dist * (-LOG2E))


def finish(ls_ref, var_ref, first, rows, cols, rnorm, o_hbm, stage, sem1, sem0):
    rc = rows.shape[3]
    half = NC * rc
    send = pltpu.make_async_copy(first, o_hbm.at[1], sem1)
    send.start()
    ls = ls_ref[0]
    var = var_ref[0]
    scale = 5.0 / (ls * ls)
    cn = col_norm(cols, 0)

    def out_copy(i, h):
        at = pl.ds(pl.multiple_of(h * half + i * rc, rc), rc)
        return pltpu.make_async_copy(stage.at[at], o_hbm.at[0, at], sem0.at[i, h])

    @pl.loop(0, NC)
    def _(i):
        out = values(gathered(rows, i), rnorm[i], cols[0], cn, scale, var)
        for h in (0, 1):
            stage[pl.ds(pl.multiple_of(h * half + i * rc, rc), rc), :] = out[h * rc:(h + 1) * rc]
            out_copy(i, h).start()

    send.wait()

    @pl.loop(0, NC)
    def _(i):
        for h in (0, 1):
            out_copy(i, h).wait()


def kernel(off_ref, ls_ref, var_ref, x_hbm, o_ref, rows, cols, rnorm, xv, tr, rot1, rot2, mine, cnorm,
           in_sem, s_sw, r_sw, s_row, r_row, s_sib, r_sib, s_rot, r_rot, s_tp, r_tp, s_cz, r_cz, s_cx, r_cx):
    r = lax.axis_index("prow")
    q = lax.axis_index("pcol")
    x = r % 4
    zl = r // 4
    c = q % 2
    oc = 1 - c
    y = (q // 2) % 4
    zh = q // 8
    rc = rows.shape[3]
    half = NC * rc

    def at_q(zhi, yy, cc):
        return {"prow": r, "pcol": zhi * 8 + yy * 2 + cc}

    def at_r(rr):
        return {"prow": rr, "pcol": q}

    sib = at_q(zh, y, oc)
    up = at_q(zh, (y + 1) % 4, c)
    down = at_q(zh, (y + 3) % 4, c)
    across = at_q(1 - zh, y, c)
    flip = {"prow": q, "pcol": r}

    load = pltpu.make_async_copy(x_hbm, xv, in_sem)
    load.start()
    bar = pltpu.get_barrier_semaphore()
    for d in (sib, up, down, across):
        pl.semaphore_signal(bar, inc=1, device_id=d, device_id_type=MESH)
    for d in range(1, 16):
        pl.semaphore_signal(bar, inc=1, device_id=at_r((r + d) % 16), device_id_type=MESH)

    @pl.when(q != r)
    def _():
        pl.semaphore_signal(bar, inc=1, device_id=flip, device_id_type=MESH)

    load.wait()
    off0 = off_ref[0]
    slot = lax.shift_right_logical(off0 - r + 15, 4)
    rot1[0] = pick([xv[:, s * TB:(s + 2) * TB] for s in range(xv.shape[1] // TB - 1)], slot)
    mine[1] = xv[:, xv.shape[1] - 2 * TB:]
    pl.semaphore_wait(bar, 19 + (q != r).astype(jnp.int32))

    def swap(i):
        return pltpu.make_async_remote_copy(
            xv.at[:, pl.ds(pl.multiple_of(oc * half + i * rc, rc), rc)], tr.at[i, c],
            s_sw.at[i], r_sw.at[i], device_id=sib, device_id_type=MESH)

    @pl.loop(0, NC)
    def _(i):
        swap(i).start()

    def turn(stage, d):
        buf = rot1 if stage == 0 else rot2
        step = 1 if stage == 0 else 4
        return pltpu.make_async_remote_copy(
            buf.at[0], buf.at[d], s_rot.at[stage, d - 1], r_rot.at[stage, d - 1],
            device_id=at_r((r + 16 - step * d) % 16), device_id_type=MESH)

    def flipped(p):
        return pltpu.make_async_remote_copy(
            mine.at[p], cols.at[p, zh * 2 + y // 2, (y % 2) * 2 + c], s_tp.at[p], r_tp.at[p],
            device_id=flip, device_id_type=MESH)

    def flip_start(p):
        @pl.when(q != r)
        def _():
            flipped(p).start()

        @pl.when(q == r)
        def _():
            cols[p, zl, x] = mine[p]

    def flip_wait(p):
        @pl.when(q != r)
        def _():
            flipped(p).wait_recv()

    def col_z(p, d):
        return pltpu.make_async_remote_copy(
            cols.at[p, zl, x], cols.at[p, zl, x], s_cz.at[p, d - 1], r_cz.at[p, d - 1],
            device_id=at_r((r + 4 * d) % 16), device_id_type=MESH)

    def col_z_wait(p, d):
        src = cols.at[p, (zl + 4 - d) % 4, x]
        return pltpu.make_async_remote_copy(
            src, src, s_cz.at[p, d - 1], r_cz.at[p, d - 1],
            device_id=at_r((r + 4 * d) % 16), device_id_type=MESH)

    def col_x(p, d):
        return pltpu.make_async_remote_copy(
            cols.at[p, :, x], cols.at[p, :, x], s_cx.at[p, d - 1], r_cx.at[p, d - 1],
            device_id=at_r(zl * 4 + (x + d) % 4), device_id_type=MESH)

    def col_x_wait(p, d):
        src = cols.at[p, :, (x + 4 - d) % 4]
        return pltpu.make_async_remote_copy(
            src, src, s_cx.at[p, d - 1], r_cx.at[p, d - 1],
            device_id=at_r(zl * 4 + (x + d) % 4), device_id_type=MESH)

    if True:
        for d in (1, 2, 3):
            turn(0, d).start()
        flip_start(1)

    UP, DOWN, FUP, ACROSS = 0, 1, 2, 8

    def base(g):
        return (zh if g == 0 else 1 - zh) * 4

    def row_copy(kind, i, block, lo, n, to):
        ref = rows.at[c, i, block, pl.ds(lo, n)]
        return pltpu.make_async_remote_copy(ref, ref, s_row.at[kind, i], r_row.at[kind, i],
                                            device_id=to, device_id_type=MESH)

    def send_up(g, i):
        return row_copy(4 * g + UP, i, base(g) + y, 0, rc, up)

    def send_down(g, i):
        return row_copy(4 * g + DOWN, i, base(g) + y, 0, rc, down)

    def send_across(i):
        return row_copy(ACROSS, i, base(0) + y, 0, rc, across)

    def passing(g, i, each):
        @pl.when((i + g) % 2 == 0)
        def _():
            each(row_copy(4 * g + FUP, i, base(g) + (y + 3) % 4, 0, rc, up))

        @pl.when((i + g) % 2 == 1)
        def _():
            each(row_copy(4 * g + FUP, i, base(g) + (y + 1) % 4, 0, rc, down))

    def pass_on(g, i):
        passing(g, i, lambda copy: copy.start())

    def got_up(g, i):
        return row_copy(4 * g + UP, i, base(g) + (y + 3) % 4, 0, rc, up)

    def got_down(g, i):
        return row_copy(4 * g + DOWN, i, base(g) + (y + 1) % 4, 0, rc, down)

    def got_across(i):
        return row_copy(ACROSS, i, base(1) + y, 0, rc, across)

    def got_passed(g, i):
        return row_copy(4 * g + FUP, i, base(g) + (y + 2) % 4, 0, rc, up)

    def share(g, i, h):
        ref = rows.at[h, i, pl.ds(base(g), 4)]
        return pltpu.make_async_remote_copy(ref, ref, s_sib.at[g, i], r_sib.at[g, i],
                                            device_id=sib, device_id_type=MESH)

    own = zh * 4 + y

    def launch(i):
        tr[i, c] = xv[:, pl.ds(pl.multiple_of(c * half + i * rc, rc), rc)]
        pltpu.make_async_remote_copy(tr.at[i, oc], tr.at[i, oc], s_sw.at[i], r_sw.at[i],
                                     device_id=sib, device_id_type=MESH).wait_recv()
        rows[c, i, own] = tr[i].reshape(2 * tr.shape[2], rc).T
        send_up(0, i).start()
        send_down(0, i).start()

    @pl.loop(0, AHEAD)
    def _(i):
        launch(i)

    if True:
        for d in (1, 2, 3):
            turn(0, d).wait_recv()
        rot2[0] = pick([rot1[d] for d in range(4)], lax.bitwise_and(off0, 3))
        for d in (1, 2, 3):
            turn(1, d).start()

    ls = ls_ref[0]
    var = var_ref[0]
    scale = 5.0 / (ls * ls)

    def norms(p):
        for d in (1, 2, 3):
            col_x_wait(p, d).wait_recv()
        if p == 1:
            cnorm[p] = col_norm(cols, p)

    def compute(i):
        lhs = gathered(rows, i)
        rnorm[i] = jnp.sum(jnp.square(lhs.astype(F32)), axis=1, keepdims=True)
        out = values(lhs, rnorm[i], cols[1], cnorm[1], scale, var)
        for h in (0, 1):
            o_ref[pl.ds(pl.multiple_of(h * half + i * rc, rc), rc), :] = out[h * rc:(h + 1) * rc]

    def own_pass(lo, hi):
        @pl.loop(lo, hi)
        def _(i):
            got_up(0, i).wait_recv()
            got_down(0, i).wait_recv()
            pass_on(0, i)

    @pl.loop(0, ZWIN)
    def _(i):
        send_across(i).start()

    def panel1_z():
        flip_wait(1)
        for d in (1, 2, 3):
            col_z(1, d).start()

    def panel0_flip():
        for d in (1, 2, 3):
            turn(1, d).wait_recv()
        mine[0] = pick([rot2[d] for d in range(4)], lax.bitwise_and(lax.shift_right_logical(off0, 2), 3))
        flip_start(0)

    own_pass(0, OWN[0])
    if EARLY[0] < 0:
        panel1_z()
    if EARLY[1] < 0:
        panel0_flip()
    own_pass(OWN[0], OWN[1])

    @pl.loop(0, NC + LAG[3])
    def _(s):
        @pl.when(s < NC)
        def _():
            got_across(s).wait_recv()
            send_up(1, s).start()
            send_down(1, s).start()

        if True:
            pl.when(s == EARLY[0])(panel1_z)
            pl.when(s == EARLY[1])(panel0_flip)

            @pl.when(s == STEPS[0])
            def _():
                for d in (1, 2, 3):
                    col_z_wait(1, d).wait_recv()
                for d in (1, 2, 3):
                    col_x(1, d).start()

            @pl.when(s == STEPS[1])
            def _():
                flip_wait(0)
                for d in (1, 2, 3):
                    col_z(0, d).start()

            @pl.when(s == STEPS[2])
            def _():
                for d in (1, 2, 3):
                    col_z_wait(0, d).wait_recv()
                for d in (1, 2, 3):
                    col_x(0, d).start()

        @pl.when(s + ZWIN < NC)
        def _():
            send_across(s + ZWIN).start()

        for k in range(2, len(OWN)):
            @pl.when(s == k - 2)
            def _():
                own_pass(OWN[k - 1], OWN[k])

        b = s - LAG[0]

        @pl.when((b >= 0) & (b < NC))
        def _():
            got_up(1, b).wait_recv()
            got_down(1, b).wait_recv()
            pass_on(1, b)

        e = s - LAG[1]

        @pl.when((e >= 0) & (e < NC))
        def _():
            got_passed(0, e).wait_recv()
            share(0, e, c).start()

        f = s - LAG[2]

        @pl.when((f >= 0) & (f < NC))
        def _():
            got_passed(1, f).wait_recv()
            share(1, f, c).start()

        @pl.when(s == CS1)
        def _():
            norms(1)

        for k in (0, 1):
            g = jnp.where(s < 2 * CS1 - LAG[3], 2 * (s - CS1) + k, s - LAG[3] if k == 0 else -1)

            @pl.when((g >= 0) & (s >= CS1))
            def _():
                share(0, g, oc).wait_recv()
                share(1, g, oc).wait_recv()
                compute(g)

    norms(0)

    if True:
        for stage in (0, 1):
            for d in (1, 2, 3):
                turn(stage, d).wait_send()
        for p in (0, 1):
            @pl.when(q != r)
            def _():
                flipped(p).wait_send()

            for d in (1, 2, 3):
                col_z(p, d).wait_send()
                col_x(p, d).wait_send()

    @pl.loop(0, NC)
    def _(i):
        swap(i).wait_send()
        send_across(i).wait_send()
        for g in (0, 1):
            send_up(g, i).wait_send()
            send_down(g, i).wait_send()
            passing(g, i, lambda copy: copy.wait_send())
            share(g, i, c).wait_send()


def on_device(features, panel_offsets, length_scale, variance):
    pts, width = features.shape
    rc = pts // (2 * NC)
    smem = pl.BlockSpec(memory_space=pltpu.SMEM)
    dma = pltpu.SemaphoreType.DMA
    vmem = pl.BlockSpec(memory_space=pltpu.VMEM)
    first, rows, cols, rnorm = pl.pallas_call(
        kernel,
        out_shape=[
            pltpu.VMEM((pts, 2 * TB), F32),
            pltpu.VMEM((2, NC, 8, rc, 2 * width), BF16),
            pltpu.VMEM((2, 4, 4, width, 2 * TB), BF16),
            pltpu.VMEM((NC, 2 * rc, 1), F32),
        ],
        in_specs=[smem, smem, smem, pl.BlockSpec(memory_space=pl.ANY)],
        out_specs=[vmem] * 4,
        scratch_shapes=[
            pltpu.VMEM((width, pts), BF16),
            pltpu.VMEM((NC, 2, width, rc), BF16),
            pltpu.VMEM((4, width, 2 * TB), BF16),
            pltpu.VMEM((4, width, 2 * TB), BF16),
            pltpu.VMEM((2, width, 2 * TB), BF16),
            pltpu.VMEM((2, 1, 2 * TB), F32),
            dma, dma((NC,)), dma((NC,)), dma((9, NC)), dma((9, NC)), dma((2, NC)), dma((2, NC)),
            dma((2, 3)), dma((2, 3)), dma((2,)), dma((2,)), dma((2, 3)), dma((2, 3)), dma((2, 3)), dma((2, 3)),
        ],
        compiler_params=pltpu.CompilerParams(
            collective_id=0, has_side_effects=True, vmem_limit_bytes=40 * 2**20),
        cost_estimate=pl.CostEstimate(flops=2 * pts * 1024 * 512, bytes_accessed=9 * 2**20, transcendentals=0),
        name="panels",
    )(panel_offsets, length_scale, variance, features.T)
    return pl.pallas_call(
        finish,
        out_shape=jax.ShapeDtypeStruct((2, pts, 2 * TB), F32),
        in_specs=[smem, smem, vmem, vmem, vmem, vmem],
        out_specs=pl.BlockSpec(memory_space=pl.ANY),
        scratch_shapes=[pltpu.VMEM((pts, 2 * TB), F32), dma, dma((NC, 2))],
        compiler_params=pltpu.CompilerParams(vmem_limit_bytes=24 * 2**20),
        name="finish",
    )(length_scale, variance, first, rows, cols, rnorm)


def solution(mesh):
    return jax.shard_map(
        on_device,
        mesh=mesh,
        in_specs=(P("prow", "pcol"), P(), P(), P()),
        out_specs=P(None, "prow", "pcol"),
        check_vma=False,
    )
```

```python
import functools

import jax
import jax.numpy as jnp
from jax import lax
from jax.experimental import pallas as pl
from jax.experimental.pallas import tpu as pltpu
from jax.sharding import PartitionSpec as P

TB = 128
NC = 8
AHEAD = 8
LAG = (2, 3, 4, 5)
ZWIN = 3
EARLY = (-1, 0)
OWN = (3, 3, 6, 8)
STEPS = (1, 3, 6)
CS1 = 6
LOG2E = 1.4426950408889634
MESH = pl.DeviceIdType.MESH
BF16 = jnp.bfloat16
F32 = jnp.float32


def pick(options, which):
    which = jnp.full(options[0].shape, which, jnp.int32)
    out = options[0].astype(F32)
    for n, option in enumerate(options[1:], 1):
        out = jnp.where(which == n, option.astype(F32), out)
    return out.astype(BF16)


def gathered(rows, i):
    return jnp.concatenate([
        jnp.concatenate([rows[h, i, k] for k in range(8)], axis=1) for h in (0, 1)], axis=0)


def col_norm(cols, p):
    total = jnp.zeros((1, 2 * TB), F32)
    for a in range(4):
        for b in range(4):
            total += jnp.sum(jnp.square(cols[p, a, b].astype(F32)), axis=0, keepdims=True)
    return total


def values(lhs, rn, columns, cn, scale, var):
    gram = jnp.dot(lhs, columns.reshape(lhs.shape[1], 2 * TB), preferred_element_type=F32)
    sq = jnp.maximum((rn * scale + cn * scale) - (2.0 * scale) * gram, 1e-30)
    dist = sq * lax.rsqrt(sq)
    return (var * (1.0 + dist + sq * (1.0 / 3.0))) * jnp.exp2(dist * (-LOG2E))


def finish(ls_ref, var_ref, first, rows, cols, rnorm, o_hbm, stage, sem1, sem0):
    rc = rows.shape[3]
    half = NC * rc
    send = pltpu.make_async_copy(first, o_hbm.at[1], sem1)
    send.start()
    ls = ls_ref[0]
    var = var_ref[0]
    scale = 5.0 / (ls * ls)
    cn = col_norm(cols, 0)

    def out_copy(i, h):
        at = pl.ds(pl.multiple_of(h * half + i * rc, rc), rc)
        return pltpu.make_async_copy(stage.at[at], o_hbm.at[0, at], sem0.at[i, h])

    @pl.loop(0, NC // 4)
    def _(j):
        parts = [4 * j + k for k in range(4)]
        outs = [values(gathered(rows, i), rnorm[i], cols[0], cn, scale, var) for i in parts]
        for i, out in zip(parts, outs):
            for h in (0, 1):
                stage[pl.ds(pl.multiple_of(h * half + i * rc, rc), rc), :] = out[h * rc:(h + 1) * rc]
                out_copy(i, h).start()

    send.wait()

    @pl.loop(0, NC)
    def _(i):
        for h in (0, 1):
            out_copy(i, h).wait()


def kernel(off_ref, ls_ref, var_ref, x_hbm, o_ref, rows, cols, rnorm, xv, tr, rot1, rot2, mine, cnorm,
           in_sem, s_sw, r_sw, s_row, r_row, s_sib, r_sib, s_rot, r_rot, s_tp, r_tp, s_cz, r_cz, s_cx, r_cx):
    r = lax.axis_index("prow")
    q = lax.axis_index("pcol")
    x = r % 4
    zl = r // 4
    c = q % 2
    oc = 1 - c
    y = (q // 2) % 4
    zh = q // 8
    rc = rows.shape[3]
    half = NC * rc

    def at_q(zhi, yy, cc):
        return {"prow": r, "pcol": zhi * 8 + yy * 2 + cc}

    def at_r(rr):
        return {"prow": rr, "pcol": q}

    sib = at_q(zh, y, oc)
    up = at_q(zh, (y + 1) % 4, c)
    down = at_q(zh, (y + 3) % 4, c)
    across = at_q(1 - zh, y, c)
    flip = {"prow": q, "pcol": r}

    load = pltpu.make_async_copy(x_hbm, xv, in_sem)
    load.start()
    bar = pltpu.get_barrier_semaphore()
    for d in (sib, up, down, across):
        pl.semaphore_signal(bar, inc=1, device_id=d, device_id_type=MESH)
    for d in range(1, 16):
        pl.semaphore_signal(bar, inc=1, device_id=at_r((r + d) % 16), device_id_type=MESH)

    @pl.when(q != r)
    def _():
        pl.semaphore_signal(bar, inc=1, device_id=flip, device_id_type=MESH)

    load.wait()
    off0 = off_ref[0]
    slot = lax.shift_right_logical(off0 - r + 15, 4)
    rot1[0] = pick([xv[:, s * TB:(s + 2) * TB] for s in range(xv.shape[1] // TB - 1)], slot)
    mine[1] = xv[:, xv.shape[1] - 2 * TB:]
    pl.semaphore_wait(bar, 19 + (q != r).astype(jnp.int32))

    def swap(i):
        return pltpu.make_async_remote_copy(
            xv.at[:, pl.ds(pl.multiple_of(oc * half + i * rc, rc), rc)], tr.at[i, c],
            s_sw.at[i], r_sw.at[i], device_id=sib, device_id_type=MESH)

    @pl.loop(0, NC)
    def _(i):
        swap(i).start()

    def turn(stage, d):
        buf = rot1 if stage == 0 else rot2
        step = 1 if stage == 0 else 4
        return pltpu.make_async_remote_copy(
            buf.at[0], buf.at[d], s_rot.at[stage, d - 1], r_rot.at[stage, d - 1],
            device_id=at_r((r + 16 - step * d) % 16), device_id_type=MESH)

    def flipped(p):
        return pltpu.make_async_remote_copy(
            mine.at[p], cols.at[p, zh * 2 + y // 2, (y % 2) * 2 + c], s_tp.at[p], r_tp.at[p],
            device_id=flip, device_id_type=MESH)

    def flip_start(p):
        @pl.when(q != r)
        def _():
            flipped(p).start()

        @pl.when(q == r)
        def _():
            cols[p, zl, x] = mine[p]

    def flip_wait(p):
        @pl.when(q != r)
        def _():
            flipped(p).wait_recv()

    def col_z(p, d):
        return pltpu.make_async_remote_copy(
            cols.at[p, zl, x], cols.at[p, zl, x], s_cz.at[p, d - 1], r_cz.at[p, d - 1],
            device_id=at_r((r + 4 * d) % 16), device_id_type=MESH)

    def col_z_wait(p, d):
        src = cols.at[p, (zl + 4 - d) % 4, x]
        return pltpu.make_async_remote_copy(
            src, src, s_cz.at[p, d - 1], r_cz.at[p, d - 1],
            device_id=at_r((r + 4 * d) % 16), device_id_type=MESH)

    def col_x(p, d):
        return pltpu.make_async_remote_copy(
            cols.at[p, :, x], cols.at[p, :, x], s_cx.at[p, d - 1], r_cx.at[p, d - 1],
            device_id=at_r(zl * 4 + (x + d) % 4), device_id_type=MESH)

    def col_x_wait(p, d):
        src = cols.at[p, :, (x + 4 - d) % 4]
        return pltpu.make_async_remote_copy(
            src, src, s_cx.at[p, d - 1], r_cx.at[p, d - 1],
            device_id=at_r(zl * 4 + (x + d) % 4), device_id_type=MESH)

    if True:
        for d in (1, 2, 3):
            turn(0, d).start()
        flip_start(1)

    UP, DOWN, FUP, ACROSS = 0, 1, 2, 8

    def base(g):
        return (zh if g == 0 else 1 - zh) * 4

    def row_copy(kind, i, block, lo, n, to):
        ref = rows.at[c, i, block, pl.ds(lo, n)]
        return pltpu.make_async_remote_copy(ref, ref, s_row.at[kind, i], r_row.at[kind, i],
                                            device_id=to, device_id_type=MESH)

    def send_up(g, i):
        return row_copy(4 * g + UP, i, base(g) + y, 0, rc, up)

    def send_down(g, i):
        return row_copy(4 * g + DOWN, i, base(g) + y, 0, rc, down)

    def send_across(i):
        return row_copy(ACROSS, i, base(0) + y, 0, rc, across)

    def passing(g, i, each):
        @pl.when((i + g) % 2 == 0)
        def _():
            each(row_copy(4 * g + FUP, i, base(g) + (y + 3) % 4, 0, rc, up))

        @pl.when((i + g) % 2 == 1)
        def _():
            each(row_copy(4 * g + FUP, i, base(g) + (y + 1) % 4, 0, rc, down))

    def pass_on(g, i):
        passing(g, i, lambda copy: copy.start())

    def got_up(g, i):
        return row_copy(4 * g + UP, i, base(g) + (y + 3) % 4, 0, rc, up)

    def got_down(g, i):
        return row_copy(4 * g + DOWN, i, base(g) + (y + 1) % 4, 0, rc, down)

    def got_across(i):
        return row_copy(ACROSS, i, base(1) + y, 0, rc, across)

    def got_passed(g, i):
        return row_copy(4 * g + FUP, i, base(g) + (y + 2) % 4, 0, rc, up)

    def share(g, i, h):
        ref = rows.at[h, i, pl.ds(base(g), 4)]
        return pltpu.make_async_remote_copy(ref, ref, s_sib.at[g, i], r_sib.at[g, i],
                                            device_id=sib, device_id_type=MESH)

    own = zh * 4 + y

    def launch(i):
        tr[i, c] = xv[:, pl.ds(pl.multiple_of(c * half + i * rc, rc), rc)]
        pltpu.make_async_remote_copy(tr.at[i, oc], tr.at[i, oc], s_sw.at[i], r_sw.at[i],
                                     device_id=sib, device_id_type=MESH).wait_recv()
        rows[c, i, own] = tr[i].reshape(2 * tr.shape[2], rc).T
        send_up(0, i).start()
        send_down(0, i).start()

    @pl.loop(0, AHEAD)
    def _(i):
        launch(i)

    if True:
        for d in (1, 2, 3):
            turn(0, d).wait_recv()
        rot2[0] = pick([rot1[d] for d in range(4)], lax.bitwise_and(off0, 3))
        for d in (1, 2, 3):
            turn(1, d).start()

    ls = ls_ref[0]
    var = var_ref[0]
    scale = 5.0 / (ls * ls)

    def norms(p):
        for d in (1, 2, 3):
            col_x_wait(p, d).wait_recv()
        if p == 1:
            cnorm[p] = col_norm(cols, p)

    def compute(i):
        lhs = gathered(rows, i)
        rnorm[i] = jnp.sum(jnp.square(lhs.astype(F32)), axis=1, keepdims=True)
        out = values(lhs, rnorm[i], cols[1], cnorm[1], scale, var)
        for h in (0, 1):
            o_ref[pl.ds(pl.multiple_of(h * half + i * rc, rc), rc), :] = out[h * rc:(h + 1) * rc]

    def own_pass(lo, hi):
        @pl.loop(lo, hi)
        def _(i):
            got_up(0, i).wait_recv()
            got_down(0, i).wait_recv()
            pass_on(0, i)

    @pl.loop(0, ZWIN)
    def _(i):
        send_across(i).start()

    def panel1_z():
        flip_wait(1)
        for d in (1, 2, 3):
            col_z(1, d).start()

    def panel0_flip():
        for d in (1, 2, 3):
            turn(1, d).wait_recv()
        mine[0] = pick([rot2[d] for d in range(4)], lax.bitwise_and(lax.shift_right_logical(off0, 2), 3))
        flip_start(0)

    own_pass(0, OWN[0])
    if EARLY[0] < 0:
        panel1_z()
    if EARLY[1] < 0:
        panel0_flip()
    own_pass(OWN[0], OWN[1])

    @pl.loop(0, NC + LAG[3])
    def _(s):
        @pl.when(s < NC)
        def _():
            got_across(s).wait_recv()
            send_up(1, s).start()
            send_down(1, s).start()

        if True:
            pl.when(s == EARLY[0])(panel1_z)
            pl.when(s == EARLY[1])(panel0_flip)

            @pl.when(s == STEPS[0])
            def _():
                for d in (1, 2, 3):
                    col_z_wait(1, d).wait_recv()
                for d in (1, 2, 3):
                    col_x(1, d).start()

            @pl.when(s == STEPS[1])
            def _():
                flip_wait(0)
                for d in (1, 2, 3):
                    col_z(0, d).start()

            @pl.when(s == STEPS[2])
            def _():
                for d in (1, 2, 3):
                    col_z_wait(0, d).wait_recv()
                for d in (1, 2, 3):
                    col_x(0, d).start()

        @pl.when(s + ZWIN < NC)
        def _():
            send_across(s + ZWIN).start()

        for k in range(2, len(OWN)):
            @pl.when(s == k - 2)
            def _():
                own_pass(OWN[k - 1], OWN[k])

        b = s - LAG[0]

        @pl.when((b >= 0) & (b < NC))
        def _():
            got_up(1, b).wait_recv()
            got_down(1, b).wait_recv()
            pass_on(1, b)

        e = s - LAG[1]

        @pl.when((e >= 0) & (e < NC))
        def _():
            got_passed(0, e).wait_recv()
            share(0, e, c).start()

        f = s - LAG[2]

        @pl.when((f >= 0) & (f < NC))
        def _():
            got_passed(1, f).wait_recv()
            share(1, f, c).start()

        @pl.when(s == CS1)
        def _():
            norms(1)

        for k in (0, 1):
            g = jnp.where(s < 2 * CS1 - LAG[3], 2 * (s - CS1) + k, s - LAG[3] if k == 0 else -1)

            @pl.when((g >= 0) & (s >= CS1))
            def _():
                share(0, g, oc).wait_recv()
                share(1, g, oc).wait_recv()
                compute(g)

    norms(0)

    if True:
        for stage in (0, 1):
            for d in (1, 2, 3):
                turn(stage, d).wait_send()
        for p in (0, 1):
            @pl.when(q != r)
            def _():
                flipped(p).wait_send()

            for d in (1, 2, 3):
                col_z(p, d).wait_send()
                col_x(p, d).wait_send()

    @pl.loop(0, NC)
    def _(i):
        swap(i).wait_send()
        send_across(i).wait_send()
        for g in (0, 1):
            send_up(g, i).wait_send()
            send_down(g, i).wait_send()
            passing(g, i, lambda copy: copy.wait_send())
            share(g, i, c).wait_send()


def on_device(features, panel_offsets, length_scale, variance):
    pts, width = features.shape
    rc = pts // (2 * NC)
    smem = pl.BlockSpec(memory_space=pltpu.SMEM)
    dma = pltpu.SemaphoreType.DMA
    vmem = pl.BlockSpec(memory_space=pltpu.VMEM)
    first, rows, cols, rnorm = pl.pallas_call(
        kernel,
        out_shape=[
            pltpu.VMEM((pts, 2 * TB), F32),
            pltpu.VMEM((2, NC, 8, rc, 2 * width), BF16),
            pltpu.VMEM((2, 4, 4, width, 2 * TB), BF16),
            pltpu.VMEM((NC, 2 * rc, 1), F32),
        ],
        in_specs=[smem, smem, smem, pl.BlockSpec(memory_space=pl.ANY)],
        out_specs=[vmem] * 4,
        scratch_shapes=[
            pltpu.VMEM((width, pts), BF16),
            pltpu.VMEM((NC, 2, width, rc), BF16),
            pltpu.VMEM((4, width, 2 * TB), BF16),
            pltpu.VMEM((4, width, 2 * TB), BF16),
            pltpu.VMEM((2, width, 2 * TB), BF16),
            pltpu.VMEM((2, 1, 2 * TB), F32),
            dma, dma((NC,)), dma((NC,)), dma((9, NC)), dma((9, NC)), dma((2, NC)), dma((2, NC)),
            dma((2, 3)), dma((2, 3)), dma((2,)), dma((2,)), dma((2, 3)), dma((2, 3)), dma((2, 3)), dma((2, 3)),
        ],
        compiler_params=pltpu.CompilerParams(
            collective_id=0, has_side_effects=True, vmem_limit_bytes=40 * 2**20),
        cost_estimate=pl.CostEstimate(flops=2 * pts * 1024 * 512, bytes_accessed=9 * 2**20, transcendentals=0),
        name="panels",
    )(panel_offsets, length_scale, variance, features.T)
    return pl.pallas_call(
        finish,
        out_shape=jax.ShapeDtypeStruct((2, pts, 2 * TB), F32),
        in_specs=[smem, smem, vmem, vmem, vmem, vmem],
        out_specs=pl.BlockSpec(memory_space=pl.ANY),
        scratch_shapes=[pltpu.VMEM((pts, 2 * TB), F32), dma, dma((NC, 2))],
        compiler_params=pltpu.CompilerParams(vmem_limit_bytes=24 * 2**20),
        name="finish",
    )(length_scale, variance, first, rows, cols, rnorm)


def solution(mesh):
    return jax.shard_map(
        on_device,
        mesh=mesh,
        in_specs=(P("prow", "pcol"), P(), P(), P()),
        out_specs=P(None, "prow", "pcol"),
        check_vma=False,
    )
```

```python
import functools

import jax
import jax.numpy as jnp
from jax import lax
from jax.experimental import pallas as pl
from jax.experimental.pallas import tpu as pltpu
from jax.sharding import PartitionSpec as P

TB = 128
NC = 8
AHEAD = 8
LAG = (2, 3, 4, 5)
ZWIN = 3
EARLY = (-1, 0)
OWN = (3, 3, 6, 8)
STEPS = (1, 3, 6)
CS1 = 6
LOG2E = 1.4426950408889634
MESH = pl.DeviceIdType.MESH
BF16 = jnp.bfloat16
F32 = jnp.float32


def pick(options, which):
    which = jnp.full(options[0].shape, which, jnp.int32)
    out = options[0].astype(F32)
    for n, option in enumerate(options[1:], 1):
        out = jnp.where(which == n, option.astype(F32), out)
    return out.astype(BF16)


def gathered(rows, i):
    return jnp.concatenate([
        jnp.concatenate([rows[h, i, k] for k in range(8)], axis=1) for h in (0, 1)], axis=0)


def col_norm(cols, p):
    total = jnp.zeros((1, 2 * TB), F32)
    for a in range(4):
        for b in range(4):
            total += jnp.sum(jnp.square(cols[p, a, b].astype(F32)), axis=0, keepdims=True)
    return total


def values(lhs, rn, columns, cn, scale, var):
    gram = jnp.dot(lhs, columns.reshape(lhs.shape[1], 2 * TB), preferred_element_type=F32)
    sq = jnp.maximum((rn * scale + cn * scale) - (2.0 * scale) * gram, 1e-30)
    dist = sq * lax.rsqrt(sq)
    return (var * (1.0 + dist + sq * (1.0 / 3.0))) * jnp.exp2(dist * (-LOG2E))


def finish(ls_ref, var_ref, first, rows, cols, rnorm, o_hbm, stage, sem1, sem0):
    rc = rows.shape[3]
    half = NC * rc
    send = pltpu.make_async_copy(first, o_hbm.at[1], sem1)
    send.start()
    ls = ls_ref[0]
    var = var_ref[0]
    scale = 5.0 / (ls * ls)
    cn = col_norm(cols, 0)

    def out_copy(i, h):
        at = pl.ds(pl.multiple_of(h * half + i * rc, rc), rc)
        return pltpu.make_async_copy(stage.at[at], o_hbm.at[0, at], sem0.at[i, h])

    @pl.loop(0, NC // 8)
    def _(j):
        parts = [8 * j + k for k in range(8)]
        outs = [values(gathered(rows, i), rnorm[i], cols[0], cn, scale, var) for i in parts]
        for i, out in zip(parts, outs):
            for h in (0, 1):
                stage[pl.ds(pl.multiple_of(h * half + i * rc, rc), rc), :] = out[h * rc:(h + 1) * rc]
                out_copy(i, h).start()

    send.wait()

    @pl.loop(0, NC)
    def _(i):
        for h in (0, 1):
            out_copy(i, h).wait()


def kernel(off_ref, ls_ref, var_ref, x_hbm, o_ref, rows, cols, rnorm, xv, tr, rot1, rot2, mine, cnorm,
           in_sem, s_sw, r_sw, s_row, r_row, s_sib, r_sib, s_rot, r_rot, s_tp, r_tp, s_cz, r_cz, s_cx, r_cx):
    r = lax.axis_index("prow")
    q = lax.axis_index("pcol")
    x = r % 4
    zl = r // 4
    c = q % 2
    oc = 1 - c
    y = (q // 2) % 4
    zh = q // 8
    rc = rows.shape[3]
    half = NC * rc

    def at_q(zhi, yy, cc):
        return {"prow": r, "pcol": zhi * 8 + yy * 2 + cc}

    def at_r(rr):
        return {"prow": rr, "pcol": q}

    sib = at_q(zh, y, oc)
    up = at_q(zh, (y + 1) % 4, c)
    down = at_q(zh, (y + 3) % 4, c)
    across = at_q(1 - zh, y, c)
    flip = {"prow": q, "pcol": r}

    load = pltpu.make_async_copy(x_hbm, xv, in_sem)
    load.start()
    bar = pltpu.get_barrier_semaphore()
    for d in (sib, up, down, across):
        pl.semaphore_signal(bar, inc=1, device_id=d, device_id_type=MESH)
    for d in range(1, 16):
        pl.semaphore_signal(bar, inc=1, device_id=at_r((r + d) % 16), device_id_type=MESH)

    @pl.when(q != r)
    def _():
        pl.semaphore_signal(bar, inc=1, device_id=flip, device_id_type=MESH)

    load.wait()
    off0 = off_ref[0]
    slot = lax.shift_right_logical(off0 - r + 15, 4)
    rot1[0] = pick([xv[:, s * TB:(s + 2) * TB] for s in range(xv.shape[1] // TB - 1)], slot)
    mine[1] = xv[:, xv.shape[1] - 2 * TB:]
    pl.semaphore_wait(bar, 19 + (q != r).astype(jnp.int32))

    def swap(i):
        return pltpu.make_async_remote_copy(
            xv.at[:, pl.ds(pl.multiple_of(oc * half + i * rc, rc), rc)], tr.at[i, c],
            s_sw.at[i], r_sw.at[i], device_id=sib, device_id_type=MESH)

    @pl.loop(0, NC)
    def _(i):
        swap(i).start()

    def turn(stage, d):
        buf = rot1 if stage == 0 else rot2
        step = 1 if stage == 0 else 4
        return pltpu.make_async_remote_copy(
            buf.at[0], buf.at[d], s_rot.at[stage, d - 1], r_rot.at[stage, d - 1],
            device_id=at_r((r + 16 - step * d) % 16), device_id_type=MESH)

    def flipped(p):
        return pltpu.make_async_remote_copy(
            mine.at[p], cols.at[p, zh * 2 + y // 2, (y % 2) * 2 + c], s_tp.at[p], r_tp.at[p],
            device_id=flip, device_id_type=MESH)

    def flip_start(p):
        @pl.when(q != r)
        def _():
            flipped(p).start()

        @pl.when(q == r)
        def _():
            cols[p, zl, x] = mine[p]

    def flip_wait(p):
        @pl.when(q != r)
        def _():
            flipped(p).wait_recv()

    def col_z(p, d):
        return pltpu.make_async_remote_copy(
            cols.at[p, zl, x], cols.at[p, zl, x], s_cz.at[p, d - 1], r_cz.at[p, d - 1],
            device_id=at_r((r + 4 * d) % 16), device_id_type=MESH)

    def col_z_wait(p, d):
        src = cols.at[p, (zl + 4 - d) % 4, x]
        return pltpu.make_async_remote_copy(
            src, src, s_cz.at[p, d - 1], r_cz.at[p, d - 1],
            device_id=at_r((r + 4 * d) % 16), device_id_type=MESH)

    def col_x(p, d):
        return pltpu.make_async_remote_copy(
            cols.at[p, :, x], cols.at[p, :, x], s_cx.at[p, d - 1], r_cx.at[p, d - 1],
            device_id=at_r(zl * 4 + (x + d) % 4), device_id_type=MESH)

    def col_x_wait(p, d):
        src = cols.at[p, :, (x + 4 - d) % 4]
        return pltpu.make_async_remote_copy(
            src, src, s_cx.at[p, d - 1], r_cx.at[p, d - 1],
            device_id=at_r(zl * 4 + (x + d) % 4), device_id_type=MESH)

    if True:
        for d in (1, 2, 3):
            turn(0, d).start()
        flip_start(1)

    UP, DOWN, FUP, ACROSS = 0, 1, 2, 8

    def base(g):
        return (zh if g == 0 else 1 - zh) * 4

    def row_copy(kind, i, block, lo, n, to):
        ref = rows.at[c, i, block, pl.ds(lo, n)]
        return pltpu.make_async_remote_copy(ref, ref, s_row.at[kind, i], r_row.at[kind, i],
                                            device_id=to, device_id_type=MESH)

    def send_up(g, i):
        return row_copy(4 * g + UP, i, base(g) + y, 0, rc, up)

    def send_down(g, i):
        return row_copy(4 * g + DOWN, i, base(g) + y, 0, rc, down)

    def send_across(i):
        return row_copy(ACROSS, i, base(0) + y, 0, rc, across)

    def passing(g, i, each):
        @pl.when((i + g) % 2 == 0)
        def _():
            each(row_copy(4 * g + FUP, i, base(g) + (y + 3) % 4, 0, rc, up))

        @pl.when((i + g) % 2 == 1)
        def _():
            each(row_copy(4 * g + FUP, i, base(g) + (y + 1) % 4, 0, rc, down))

    def pass_on(g, i):
        passing(g, i, lambda copy: copy.start())

    def got_up(g, i):
        return row_copy(4 * g + UP, i, base(g) + (y + 3) % 4, 0, rc, up)

    def got_down(g, i):
        return row_copy(4 * g + DOWN, i, base(g) + (y + 1) % 4, 0, rc, down)

    def got_across(i):
        return row_copy(ACROSS, i, base(1) + y, 0, rc, across)

    def got_passed(g, i):
        return row_copy(4 * g + FUP, i, base(g) + (y + 2) % 4, 0, rc, up)

    def share(g, i, h):
        ref = rows.at[h, i, pl.ds(base(g), 4)]
        return pltpu.make_async_remote_copy(ref, ref, s_sib.at[g, i], r_sib.at[g, i],
                                            device_id=sib, device_id_type=MESH)

    own = zh * 4 + y

    def launch(i):
        tr[i, c] = xv[:, pl.ds(pl.multiple_of(c * half + i * rc, rc), rc)]
        pltpu.make_async_remote_copy(tr.at[i, oc], tr.at[i, oc], s_sw.at[i], r_sw.at[i],
                                     device_id=sib, device_id_type=MESH).wait_recv()
        rows[c, i, own] = tr[i].reshape(2 * tr.shape[2], rc).T
        send_up(0, i).start()
        send_down(0, i).start()

    @pl.loop(0, AHEAD)
    def _(i):
        launch(i)

    if True:
        for d in (1, 2, 3):
            turn(0, d).wait_recv()
        rot2[0] = pick([rot1[d] for d in range(4)], lax.bitwise_and(off0, 3))
        for d in (1, 2, 3):
            turn(1, d).start()

    ls = ls_ref[0]
    var = var_ref[0]
    scale = 5.0 / (ls * ls)

    def norms(p):
        for d in (1, 2, 3):
            col_x_wait(p, d).wait_recv()
        if p == 1:
            cnorm[p] = col_norm(cols, p)

    def compute(i):
        lhs = gathered(rows, i)
        rnorm[i] = jnp.sum(jnp.square(lhs.astype(F32)), axis=1, keepdims=True)
        out = values(lhs, rnorm[i], cols[1], cnorm[1], scale, var)
        for h in (0, 1):
            o_ref[pl.ds(pl.multiple_of(h * half + i * rc, rc), rc), :] = out[h * rc:(h + 1) * rc]

    def own_pass(lo, hi):
        @pl.loop(lo, hi)
        def _(i):
            got_up(0, i).wait_recv()
            got_down(0, i).wait_recv()
            pass_on(0, i)

    @pl.loop(0, ZWIN)
    def _(i):
        send_across(i).start()

    def panel1_z():
        flip_wait(1)
        for d in (1, 2, 3):
            col_z(1, d).start()

    def panel0_flip():
        for d in (1, 2, 3):
            turn(1, d).wait_recv()
        mine[0] = pick([rot2[d] for d in range(4)], lax.bitwise_and(lax.shift_right_logical(off0, 2), 3))
        flip_start(0)

    own_pass(0, OWN[0])
    if EARLY[0] < 0:
        panel1_z()
    if EARLY[1] < 0:
        panel0_flip()
    own_pass(OWN[0], OWN[1])

    @pl.loop(0, NC + LAG[3])
    def _(s):
        @pl.when(s < NC)
        def _():
            got_across(s).wait_recv()
            send_up(1, s).start()
            send_down(1, s).start()

        if True:
            pl.when(s == EARLY[0])(panel1_z)
            pl.when(s == EARLY[1])(panel0_flip)

            @pl.when(s == STEPS[0])
            def _():
                for d in (1, 2, 3):
                    col_z_wait(1, d).wait_recv()
                for d in (1, 2, 3):
                    col_x(1, d).start()

            @pl.when(s == STEPS[1])
            def _():
                flip_wait(0)
                for d in (1, 2, 3):
                    col_z(0, d).start()

            @pl.when(s == STEPS[2])
            def _():
                for d in (1, 2, 3):
                    col_z_wait(0, d).wait_recv()
                for d in (1, 2, 3):
                    col_x(0, d).start()

        @pl.when(s + ZWIN < NC)
        def _():
            send_across(s + ZWIN).start()

        for k in range(2, len(OWN)):
            @pl.when(s == k - 2)
            def _():
                own_pass(OWN[k - 1], OWN[k])

        b = s - LAG[0]

        @pl.when((b >= 0) & (b < NC))
        def _():
            got_up(1, b).wait_recv()
            got_down(1, b).wait_recv()
            pass_on(1, b)

        e = s - LAG[1]

        @pl.when((e >= 0) & (e < NC))
        def _():
            got_passed(0, e).wait_recv()
            share(0, e, c).start()

        f = s - LAG[2]

        @pl.when((f >= 0) & (f < NC))
        def _():
            got_passed(1, f).wait_recv()
            share(1, f, c).start()

        @pl.when(s == CS1)
        def _():
            norms(1)

        for k in (0, 1):
            g = jnp.where(s < 2 * CS1 - LAG[3], 2 * (s - CS1) + k, s - LAG[3] if k == 0 else -1)

            @pl.when((g >= 0) & (s >= CS1))
            def _():
                share(0, g, oc).wait_recv()
                share(1, g, oc).wait_recv()
                compute(g)

    norms(0)

    if True:
        for stage in (0, 1):
            for d in (1, 2, 3):
                turn(stage, d).wait_send()
        for p in (0, 1):
            @pl.when(q != r)
            def _():
                flipped(p).wait_send()

            for d in (1, 2, 3):
                col_z(p, d).wait_send()
                col_x(p, d).wait_send()

    @pl.loop(0, NC)
    def _(i):
        swap(i).wait_send()
        send_across(i).wait_send()
        for g in (0, 1):
            send_up(g, i).wait_send()
            send_down(g, i).wait_send()
            passing(g, i, lambda copy: copy.wait_send())
            share(g, i, c).wait_send()


def on_device(features, panel_offsets, length_scale, variance):
    pts, width = features.shape
    rc = pts // (2 * NC)
    smem = pl.BlockSpec(memory_space=pltpu.SMEM)
    dma = pltpu.SemaphoreType.DMA
    vmem = pl.BlockSpec(memory_space=pltpu.VMEM)
    first, rows, cols, rnorm = pl.pallas_call(
        kernel,
        out_shape=[
            pltpu.VMEM((pts, 2 * TB), F32),
            pltpu.VMEM((2, NC, 8, rc, 2 * width), BF16),
            pltpu.VMEM((2, 4, 4, width, 2 * TB), BF16),
            pltpu.VMEM((NC, 2 * rc, 1), F32),
        ],
        in_specs=[smem, smem, smem, pl.BlockSpec(memory_space=pl.ANY)],
        out_specs=[vmem] * 4,
        scratch_shapes=[
            pltpu.VMEM((width, pts), BF16),
            pltpu.VMEM((NC, 2, width, rc), BF16),
            pltpu.VMEM((4, width, 2 * TB), BF16),
            pltpu.VMEM((4, width, 2 * TB), BF16),
            pltpu.VMEM((2, width, 2 * TB), BF16),
            pltpu.VMEM((2, 1, 2 * TB), F32),
            dma, dma((NC,)), dma((NC,)), dma((9, NC)), dma((9, NC)), dma((2, NC)), dma((2, NC)),
            dma((2, 3)), dma((2, 3)), dma((2,)), dma((2,)), dma((2, 3)), dma((2, 3)), dma((2, 3)), dma((2, 3)),
        ],
        compiler_params=pltpu.CompilerParams(
            collective_id=0, has_side_effects=True, vmem_limit_bytes=40 * 2**20),
        cost_estimate=pl.CostEstimate(flops=2 * pts * 1024 * 512, bytes_accessed=9 * 2**20, transcendentals=0),
        name="panels",
    )(panel_offsets, length_scale, variance, features.T)
    return pl.pallas_call(
        finish,
        out_shape=jax.ShapeDtypeStruct((2, pts, 2 * TB), F32),
        in_specs=[smem, smem, vmem, vmem, vmem, vmem],
        out_specs=pl.BlockSpec(memory_space=pl.ANY),
        scratch_shapes=[pltpu.VMEM((pts, 2 * TB), F32), dma, dma((NC, 2))],
        compiler_params=pltpu.CompilerParams(vmem_limit_bytes=24 * 2**20),
        name="finish",
    )(length_scale, variance, first, rows, cols, rnorm)


def solution(mesh):
    return jax.shard_map(
        on_device,
        mesh=mesh,
        in_specs=(P("prow", "pcol"), P(), P(), P()),
        out_specs=P(None, "prow", "pcol"),
        check_vma=False,
    )
```
